512 devices in a mesh: dp: 16 (over z), cls: 32 (over y, x, core).
Axes of the slice: x: 4, y: 4, z: 16, core: 2. Of those that a mesh axis runs over, the one named last changes fastest.
Arguments:
- features: bfloat16 [24576, 512], P(('dp', 'cls'))
- centers: float32 [1048576, 512], P(('dp', 'cls'))
- labels: int32 [24576], replicated, may hold values from 0 to 1048575, as said below
- sampled: int32 [512, 2], replicated, may hold values from 0 to 127, as said below
Outputs:
- losses: float32 [24576], P(('dp', 'cls'))
- feature_grad: float32 [24576, 512], P(('dp', 'cls'))
- center_grad: float32 [16384, 512], P(('dp', 'cls'))
The draws below stay inside these ranges and needn't reach their ends.
Inputs may be any that keep to these rules, and one draw needn't show every extreme that they name: Each row of sampled names 2 different blocks of 16 classes of that device's 2048 classes. `labels`: every label is a class inside a block that its owning device lists in sampled.
All inputs are finite; a program needn't handle non-finite values.
Results may differ from the reference program's by a relative error of at most 0.0046.
Values may be sent and summed in bfloat16 or wider, within the bound.
A program may use at most 64 MiB of HBM per device.

```python
import math
import jax
import jax.numpy as jnp
from jax import lax

D = 512
CLS_DEV = 2048
BLK = 16
SBLK = 2
ROWS_DEV = 48
SAMPLED = 16384
NCLASS = 1048576
ROWS_ALL = 24576
N_CLS = 32
DEVICES = 512


def scaled_field(key, base, top):
    key_rows, key_cols = jax.random.split(key)
    row_scale = jnp.exp(jax.random.uniform(key_rows, (base.shape[0], 1), jnp.float32, 0.0, top))
    col_scale = jnp.exp(jax.random.uniform(key_cols, (1, base.shape[1]), jnp.float32, 0.0, math.log(10.0)))
    return base * row_scale * col_scale


def sample_table(key):
    table_key = jax.random.fold_in(key, 5)
    keys = jax.random.split(table_key, DEVICES)
    picks = jax.vmap(lambda one_key: jax.random.permutation(one_key, CLS_DEV // BLK)[:SBLK])(keys)
    return picks.astype(jnp.int32)


def draw_features(key, part):
    key = jax.random.fold_in(key, 11)
    key_base = jax.random.fold_in(key, 0)
    key_scale = jax.random.fold_in(key, 2)
    base = jax.random.normal(key_base, (ROWS_ALL, D), jnp.float32)
    top = math.log(10.0)
    return scaled_field(key_scale, base, top).astype(jnp.bfloat16)


def draw_centers(key, part):
    key = jax.random.fold_in(key, 13)
    key_base = jax.random.fold_in(key, 0)
    key_scale = jax.random.fold_in(key, 2)
    base = jax.random.normal(key_base, (NCLASS, D), jnp.float32)
    top = math.log(10.0)
    return scaled_field(key_scale, base, top)


def draw_sampled(key, part):
    return sample_table(key)


def draw_labels(key, part):
    table = sample_table(key)
    key = jax.random.fold_in(key, 19)
    key_owner, key_slot = jax.random.split(key)
    owner = jax.random.randint(key_owner, (ROWS_ALL,), 0, DEVICES).astype(jnp.int32)
    slot = jax.random.randint(key_slot, (ROWS_ALL,), 0, SBLK * BLK).astype(jnp.int32)
    block = table[owner, slot // BLK]
    return ((owner * (CLS_DEV // BLK) + block) * BLK + slot % BLK).astype(jnp.int32)


def setup_inputs(seed: int = 0) -> dict:
    seeds = jax.random.split(jax.random.key(seed), 5)
    return {
        "features": draw_features(jax.random.fold_in(seeds[4], 71), 0),
        "centers": draw_centers(jax.random.fold_in(seeds[4], 71), 0),
        "labels": draw_labels(jax.random.fold_in(seeds[4], 71), 0),
        "sampled": draw_sampled(jax.random.fold_in(seeds[4], 71), 0),
    }


logit_scale = 64.0
cosine_margin = 0.35
norm_eps = 1e-06

def unit_rows(values):
    return values * lax.rsqrt(lax.optimization_barrier(jnp.sum(values * values, axis=-1, keepdims=True)) + norm_eps)

def reference(features, centers, labels, sampled):
    block_count = CLS_DEV // BLK
    owners = jnp.arange(DEVICES, dtype=jnp.int32)
    block_ids = (owners[:, None] * block_count + sampled.astype(jnp.int32)).reshape(-1)
    offsets = jnp.arange(BLK, dtype=jnp.int32)
    class_id = (block_ids[:, None] * BLK + offsets[None, :]).reshape(-1)
    chosen = centers.reshape(DEVICES * block_count, BLK, D)[block_ids].reshape(SAMPLED, D)
    center_full, center_back = jax.vjp(unit_rows, chosen)
    center_unit = center_full.astype(jnp.bfloat16)
    feature_full, feature_back = jax.vjp(unit_rows, features.astype(jnp.float32))
    feature_unit = feature_full.astype(jnp.bfloat16)
    group_rows = ROWS_DEV * N_CLS
    feature_blocks = feature_unit.reshape(-1, group_rows, D)
    label_blocks = labels.reshape(-1, group_rows)

    def one_block(carry, item):
        block_x, block_labels = item
        cosine = lax.dot_general(block_x, center_unit, (((1,), (1,)), ((), ())), preferred_element_type=jnp.float32)
        onehot = block_labels[:, None] == class_id[None, :]
        scores = logit_scale * cosine - logit_scale - jnp.where(onehot, logit_scale * cosine_margin, 0.0)
        expz = jnp.exp(scores)
        total = lax.optimization_barrier(jnp.sum(expz, axis=1))
        target = lax.optimization_barrier(jnp.sum(jnp.where(onehot, scores, 0.0), axis=1))
        block_loss = jnp.log(total) - target
        inverse = 1.0 / total
        grad_logit = ((expz * inverse[:, None] - onehot.astype(jnp.float32)) * logit_scale).astype(jnp.bfloat16)
        feature_term = jnp.dot(grad_logit, center_unit, preferred_element_type=jnp.float32)
        carry = carry + lax.dot_general(grad_logit, block_x, (((0,), (0,)), ((), ())), preferred_element_type=jnp.float32)
        return (carry, (block_loss, feature_term))
    center_sum, (losses, feature_terms) = lax.scan(one_block, jnp.zeros((SAMPLED, D), jnp.float32), (feature_blocks, label_blocks))
    feature_grad = feature_back(feature_terms.reshape(ROWS_ALL, D))[0]
    center_grad = center_back(center_sum)[0]
    return (losses.reshape(-1), feature_grad, center_grad)
```

```python
import functools

import jax
import jax.numpy as jnp
from jax import lax
from jax.experimental import pallas as pl
from jax.experimental.pallas import tpu as pltpu
from jax.sharding import PartitionSpec as P

MESH = pl.DeviceIdType.MESH
BLK = 16
D = 512
ROWS = 48
CLS = 32
NZ = 16
NP = 16
SIDE = 4
BLOCKS = 128
TILE_ROWS = NP * ROWS
TILE_CLS = 2 * NZ * CLS

logit_scale = 64.0
cosine_margin = 0.35
norm_eps = 1e-06

DIRECT = (4, -4, 1, -1, 2, -2)
PASS_UP = (1, 2, 3, -1)
PASS_DOWN = (-1, -2, -3, 1)
FROM_LOW = (-1, 1, 2, 3)
FROM_HIGH = (1, -1, -2, -3)


def wrap(value, size):
    return lax.rem(value + size, size)


def kernel(
    feat_ref, centers_ref, label_ref, sampled_ref,
    loss_ref, fgrad_ref, cgrad_ref,
    cbuf, chosen, xa, wa, et, gt, tot, tgt,
    sib_out, sib_in, part, part_b, relay_in, relay8, relay_out, zfin,
    fval, fout, fin1, fout2, fin2,
    csem, z_send, z_recv, s_send, s_recv, a_send, a_recv, b_send, b_recv,
    t_send, t_recv, u_send, u_recv, cs_send, cs_recv,
    r_send, r_recv, q_send, q_recv, f_send, f_recv, h_send, h_recv,
):
    z = lax.axis_index("dp")
    cls = lax.axis_index("cls")
    core = lax.rem(cls, 2)
    yx = lax.div(cls, 2)
    y = lax.div(yx, SIDE)
    x = lax.rem(yx, SIDE)
    first = jnp.where(core == 0, y, x)
    second = jnp.where(core == 0, x, y)

    def chip(p1, p2):
        return jnp.where(core == 0, p1 * SIDE + p2, p2 * SIDE + p1)

    def zdev(d):
        return (wrap(z + d, NZ), cls)

    def pdev(slot):
        return (z, slot * 2 + core)

    sibling = (z, yx * 2 + 1 - core)
    started = []

    def send(src, dst, ssem, rsem, dev):
        copy = pltpu.make_async_remote_copy(
            src_ref=src, dst_ref=dst, send_sem=ssem, recv_sem=rsem,
            device_id=dev, device_id_type=MESH,
        )
        copy.start()
        started.append(copy)

    def arrived(dst, ssem, rsem, dev):
        pltpu.make_async_remote_copy(
            src_ref=dst, dst_ref=dst, send_sem=ssem, recv_sem=rsem,
            device_id=dev, device_id_type=MESH,
        ).wait_recv()

    barrier = pltpu.get_barrier_semaphore()
    peers = [zdev(d) for d in (4, -4, 3, -3, 2, -2, 1, -1)]
    peers += [pdev(wrap(yx + j, NP)) for j in range(1, NP)]
    peers.append(sibling)
    for dev in peers:
        pl.semaphore_signal(barrier, inc=1, device_id=dev, device_id_type=MESH)
    load = pltpu.make_async_copy(centers_ref, cbuf, csem)
    load.start()

    v = feat_ref[...].astype(jnp.float32)
    fq = lax.rsqrt(jnp.sum(v * v, axis=-1, keepdims=True) + norm_eps)
    xa[yx] = (v * fq).astype(jnp.bfloat16)

    load.wait()
    owner = z * (2 * NP) + cls
    for b in range(CLS // BLK):
        chosen[b * BLK:(b + 1) * BLK, :] = cbuf[sampled_ref[owner, b]]
    c = chosen[...]
    cq = lax.rsqrt(jnp.sum(c * c, axis=-1, keepdims=True) + norm_eps)
    wa[core, z] = (c * cq).astype(jnp.bfloat16)

    pl.semaphore_wait(barrier, len(peers))

    n = 0
    for d in DIRECT:
        send(wa.at[core, z], wa.at[core, z], z_send.at[n], z_recv.at[-d % NZ], zdev(d))
        n += 1
    for j in (2, 1, 3):
        send(xa.at[yx], xa.at[yx], a_send.at[j], a_recv.at[SIDE - j], pdev(chip(wrap(first + j, SIDE), second)))
    send(wa.at[core, z], wa.at[core, z], s_send.at[0], s_recv.at[0], sibling)

    for i in range(SIDE):
        slot = chip(wrap(first + i, SIDE), second)
        if i:
            arrived(xa.at[slot], a_send.at[i], a_recv.at[i], pdev(slot))
        for j in (2, 1, 3):
            send(xa.at[slot], xa.at[slot], b_send.at[j, i], b_recv.at[SIDE - j, i],
                 pdev(chip(first, wrap(second + j, SIDE))))

    def class_arrived(d):
        slot = wrap(z + d, NZ)
        arrived(wa.at[core, slot], z_send.at[0], z_recv.at[d % NZ], zdev(d))
        send(wa.at[core, slot], wa.at[core, slot], s_send.at[d % NZ], s_recv.at[d % NZ], sibling)
        return slot

    for d, nexts in ((-4, PASS_UP), (4, PASS_DOWN)):
        slot = class_arrived(d)
        for e in nexts:
            send(wa.at[core, slot], wa.at[core, slot], z_send.at[n], z_recv.at[(d - e) % NZ], zdev(e))
            n += 1
    sign = 1 - 2 * core
    slot = wrap(z - 4 * sign, NZ)
    send(wa.at[core, slot], wa.at[core, slot], z_send.at[n], z_recv.at[8], (wrap(z + 4 * sign, NZ), cls))
    for d in (1, -1, 2, -2, 3, -3, 5, -5, 6, -6, 7, -7, 8):
        class_arrived(d)

    for i in range(SIDE):
        for j in (1, 2, 3):
            slot = chip(wrap(first + i, SIDE), wrap(second + j, SIDE))
            arrived(xa.at[slot], b_send.at[j, i], b_recv.at[j, i], pdev(slot))
    for d in range(NZ):
        slot = wrap(z + d, NZ)
        arrived(wa.at[1 - core, slot], s_send.at[d], s_recv.at[d], sibling)

    xv = xa[...].reshape(TILE_ROWS, D)
    for k in range(4):
        w = wa[k // 2, (k % 2) * 8:(k % 2) * 8 + 8].reshape(256, D)
        et[k * 256:(k + 1) * 256, :] = lax.dot_general(
            w, xv, (((1,), (1,)), ((), ())), preferred_element_type=jnp.float32
        )
    lab = label_ref[...]
    step = lax.broadcasted_iota(jnp.int32, (BLK, TILE_ROWS), 0)

    def hits(b):
        zz = lax.div(lax.rem(b, 32), 2)
        o = zz * (2 * NP) + yx * 2 + lax.div(b, 32)
        base = (o * BLOCKS + sampled_ref[o, lax.rem(b, 2)]) * BLK
        return (lab - base) == step

    def score(b, carry):
        rows = pl.ds(pl.multiple_of(b * BLK, BLK), BLK)
        hit = hits(b)
        s = logit_scale * et[rows, :] - jnp.where(hit, logit_scale * cosine_margin, 0.0)
        e = jnp.exp(s)
        et[rows, :] = e
        return carry[0] + e, carry[1] + jnp.where(hit, s, 0.0)

    zero = jnp.zeros((BLK, TILE_ROWS), jnp.float32)
    esum, tsum = lax.fori_loop(0, 2 * 32, score, (zero, zero))
    tot[0] = jnp.sum(esum, axis=0, keepdims=True)
    tgt[0] = jnp.sum(tsum, axis=0, keepdims=True)
    for j in range(1, NP):
        dev = pdev(wrap(yx + j, NP))
        send(tot.at[0], tot.at[NP - j], t_send.at[j], t_recv.at[NP - j], dev)
    for j in range(1, NP):
        dev = pdev(wrap(yx + j, NP))
        send(tgt.at[0], tgt.at[NP - j], u_send.at[j], u_recv.at[NP - j], dev)
    for j in range(1, NP):
        arrived(tot.at[j], t_send.at[j], t_recv.at[j], pdev(wrap(yx + j, NP)))
    total = tot[0]
    for j in range(1, NP):
        total = total + tot[j]
    inverse = 1.0 / total

    def grad(b, carry):
        rows = pl.ds(pl.multiple_of(b * BLK, BLK), BLK)
        hit = hits(b)
        g = (et[rows, :] * inverse - jnp.where(hit, 1.0, 0.0)) * logit_scale
        gt[rows, :] = g.astype(jnp.bfloat16)
        return carry

    def center_part(half, k):
        rows = pl.ds(pl.multiple_of(half * 512 + k * 256, 256), 256)
        return jnp.dot(gt[rows, :], xv, preferred_element_type=jnp.float32)

    other = 1 - core
    lax.fori_loop(other * 32, other * 32 + 32, grad, 0)
    for k in range(2):
        sib_out[k * 8:k * 8 + 8] = center_part(other, k).astype(jnp.bfloat16).reshape(8, CLS, D)
        send(sib_out.at[pl.ds(k * 8, 8)], sib_in.at[pl.ds(k * 8, 8)], cs_send.at[k], cs_recv.at[k], sibling)
    lax.fori_loop(core * 32, core * 32 + 32, grad, 0)
    for k in range(2):
        p = center_part(core, k).reshape(8, CLS, D)
        arrived(sib_in.at[pl.ds(k * 8, 8)], cs_send.at[k], cs_recv.at[k], sibling)
        p = p + sib_in[k * 8:k * 8 + 8].astype(jnp.float32)
        part[k * 8:k * 8 + 8] = p
        part_b[k * 8:k * 8 + 8] = p.astype(jnp.bfloat16)

    n = 0

    def give(d, dst, rsem, dev):
        nonlocal n
        send(part_b.at[wrap(z + d, NZ)], dst, r_send.at[n], rsem, dev)
        n += 1

    for side, offs in ((0, FROM_LOW), (1, FROM_HIGH)):
        for i, o in enumerate(offs):
            give((-4, 4)[side] - o, relay_in.at[side, i], r_recv.at[side * 4 + i], zdev(-o))
    give(8, relay8.at[...], r_recv.at[8], (wrap(z - 4 * sign, NZ), cls))
    for i, d in enumerate((1, -1, 2, -2)):
        give(d, zfin.at[i], q_recv.at[i], zdev(d))

    wv = wa[...].reshape(TILE_CLS, D)
    for k in range(3):
        fval[k * 256:(k + 1) * 256, :] = lax.dot_general(
            gt[:, k * 256:(k + 1) * 256], wv, (((0,), (0,)), ((), ())), preferred_element_type=jnp.float32
        )
    fout[...] = fval[...].astype(jnp.bfloat16).reshape(NP, ROWS, D)
    for i in range(SIDE):
        for j in (2, 1, 3):
            slot = chip(wrap(first + i, SIDE), wrap(second + j, SIDE))
            send(fout.at[slot], fin1.at[SIDE - j, i], f_send.at[j, i], f_recv.at[SIDE - j, i],
                 pdev(chip(first, wrap(second + j, SIDE))))

    for side, offs in ((0, FROM_LOW), (1, FROM_HIGH)):
        for i, o in enumerate(offs):
            arrived(relay_in.at[side, i], r_send.at[0], r_recv.at[side * 4 + i], zdev(o))
    arrived(relay8.at[...], r_send.at[0], r_recv.at[8], (wrap(z + 4 * sign, NZ), cls))
    for side, d in ((0, -4), (1, 4)):
        acc = part[wrap(z + d, NZ)]
        for i in range(4):
            acc = acc + relay_in[side, i].astype(jnp.float32)
        acc = acc + jnp.where(core == side, relay8[...].astype(jnp.float32), 0.0)
        relay_out[side] = acc.astype(jnp.bfloat16)
        send(relay_out.at[side], zfin.at[4 + side], q_send.at[side], q_recv.at[4 + side], zdev(d))

    own_f = None
    for i in (1, 2, 3, 0):
        slot = chip(wrap(first + i, SIDE), second)
        acc = fval[pl.ds(pl.multiple_of(slot * ROWS, 16), ROWS), :]
        for j in (1, 2, 3):
            arrived(fin1.at[j, i], f_send.at[j, i], f_recv.at[j, i], pdev(chip(first, wrap(second + j, SIDE))))
            acc = acc + fin1[j, i].astype(jnp.float32)
        if i:
            fout2[i] = acc.astype(jnp.bfloat16)
            send(fout2.at[i], fin2.at[SIDE - i], h_send.at[i], h_recv.at[SIDE - i], pdev(slot))
        else:
            own_f = acc

    for j in range(1, NP):
        arrived(tgt.at[j], u_send.at[j], u_recv.at[j], pdev(wrap(yx + j, NP)))
    target = tgt[0]
    for j in range(1, NP):
        target = target + tgt[j]
    loss_ref[...] = jnp.log(total) - target

    def back(v, q, g):
        return g * q - v * (q * q * q * jnp.sum(v * g, axis=-1, keepdims=True))

    for i in (1, 2, 3):
        arrived(fin2.at[i], h_send.at[i], h_recv.at[i], pdev(chip(wrap(first + i, SIDE), second)))
        own_f = own_f + fin2[i].astype(jnp.float32)
    fgrad_ref[...] = back(v, fq, own_f)

    own_c = part[z]
    for i, d in enumerate((-1, 1, -2, 2, 4, -4)):
        arrived(zfin.at[i], q_send.at[0], q_recv.at[i], zdev(d))
        own_c = own_c + zfin[i].astype(jnp.float32)
    cgrad_ref[...] = back(c, cq, own_c)

    for copy in started:
        copy.wait_send()


def scratch():
    bf, f32, dma = jnp.bfloat16, jnp.float32, pltpu.SemaphoreType.DMA
    vm = pltpu.VMEM
    return [
        vm((BLOCKS, BLK, D), f32), vm((CLS, D), f32), vm((NP, ROWS, D), bf), vm((2, NZ, CLS, D), bf),
        vm((TILE_CLS, TILE_ROWS), f32), vm((TILE_CLS, TILE_ROWS), bf),
        vm((NP, 1, TILE_ROWS), f32), vm((NP, 1, TILE_ROWS), f32),
        vm((NZ, CLS, D), bf), vm((NZ, CLS, D), bf), vm((NZ, CLS, D), f32), vm((NZ, CLS, D), bf),
        vm((2, 4, CLS, D), bf), vm((CLS, D), bf), vm((2, CLS, D), bf), vm((6, CLS, D), bf),
        vm((TILE_ROWS, D), f32), vm((NP, ROWS, D), bf), vm((SIDE, SIDE, ROWS, D), bf),
        vm((SIDE, ROWS, D), bf), vm((SIDE, ROWS, D), bf),
        dma, dma((NZ,)), dma((NZ,)), dma((NZ,)), dma((NZ,)), dma((SIDE,)), dma((SIDE,)),
        dma((SIDE, SIDE)), dma((SIDE, SIDE)),
        dma((NP,)), dma((NP,)), dma((NP,)), dma((NP,)), dma((2,)), dma((2,)),
        dma((13,)), dma((9,)), dma((2,)), dma((6,)), dma((SIDE, SIDE)), dma((SIDE, SIDE)), dma((SIDE,)), dma((SIDE,)),
    ]


def local(features, centers, labels, sampled):
    dp_index = lax.axis_index("dp")
    cls_index = lax.axis_index("cls")
    plane_labels = labels.reshape(NZ, NP, 2, ROWS)
    own = lax.dynamic_slice(
        plane_labels, (dp_index, 0, lax.rem(cls_index, 2), 0), (1, NP, 1, ROWS)
    ).reshape(1, TILE_ROWS)
    vmem = pl.BlockSpec(memory_space=pltpu.VMEM)
    losses, feature_grad, center_grad = pl.pallas_call(
        kernel,
        out_shape=(
            jax.ShapeDtypeStruct((1, TILE_ROWS), jnp.float32),
            jax.ShapeDtypeStruct((ROWS, D), jnp.float32),
            jax.ShapeDtypeStruct((CLS, D), jnp.float32),
        ),
        in_specs=[vmem, pl.BlockSpec(memory_space=pl.ANY), vmem, pl.BlockSpec(memory_space=pltpu.SMEM)],
        out_specs=(vmem, vmem, vmem),
        scratch_shapes=scratch(),
        compiler_params=pltpu.CompilerParams(
            collective_id=0, has_side_effects=True, vmem_limit_bytes=48 * 1024 * 1024
        ),
        name="margin_step",
    )(features, centers.reshape(BLOCKS, BLK, D), own, sampled)
    losses = lax.dynamic_slice(losses.reshape(TILE_ROWS), (lax.div(cls_index, 2) * ROWS,), (ROWS,))
    return (losses, feature_grad, center_grad)


def solution(mesh):
    placed = (P(("dp", "cls"), None), P(("dp", "cls"), None), P(), P())
    return jax.shard_map(
        local,
        mesh=mesh,
        in_specs=placed,
        out_specs=(P(("dp", "cls")), P(("dp", "cls"), None), P(("dp", "cls"), None)),
        check_vma=False,
    )
```

```python
import functools

import jax
import jax.numpy as jnp
from jax import lax
from jax.experimental import pallas as pl
from jax.experimental.pallas import tpu as pltpu
from jax.sharding import PartitionSpec as P

MESH = pl.DeviceIdType.MESH
BLK = 16
D = 512
ROWS = 48
CLS = 32
NZ = 16
NP = 16
SIDE = 4
BLOCKS = 128
TILE_ROWS = NP * ROWS
TILE_CLS = 2 * NZ * CLS

logit_scale = 64.0
cosine_margin = 0.35
norm_eps = 1e-06

ORDER = (0, 1, -1, 3, -3, 2, -2, 4, -4, 6, -6, 5, -5, 7, -7, 8)
AT = {d % NZ: p for p, d in enumerate(ORDER)}


def wrap(value, size):
    return lax.rem(value + size, size)


def kernel(
    feat_hbm, centers_hbm, label_hbm, sampled_hbm,
    loss_ref, fgrad_ref, cgrad_ref,
    feat_ref, cbuf, label_ref, sampled_ref, base_ref, chosen, xa, wa, et, gt, tot, tgt,
    sib_out, sib_in, part, part_b, near6, near8, near3, out6, out3, zfin,
    fval, fout, fin1, fout2, fin2,
    in_sem, z_send, z_recv, s_send, s_recv, a_send, a_recv, b_send, b_recv,
    t_send, t_recv, u_send, u_recv, cs_send, cs_recv,
    r_send, r_recv, q_send, q_recv, f_send, f_recv, h_send, h_recv,
):
    z = lax.axis_index("dp")
    cls = lax.axis_index("cls")
    core = lax.rem(cls, 2)
    yx = lax.div(cls, 2)
    y = lax.div(yx, SIDE)
    x = lax.rem(yx, SIDE)
    first = jnp.where(core == 0, y, x)
    second = jnp.where(core == 0, x, y)

    def chip(p1, p2):
        return jnp.where(core == 0, p1 * SIDE + p2, p2 * SIDE + p1)

    def zdev(d):
        return (wrap(z + d, NZ), cls)

    def pdev(slot):
        return (z, slot * 2 + core)

    sibling = (z, yx * 2 + 1 - core)
    started = []

    def send(src, dst, ssem, rsem, dev):
        copy = pltpu.make_async_remote_copy(
            src_ref=src, dst_ref=dst, send_sem=ssem, recv_sem=rsem,
            device_id=dev, device_id_type=MESH,
        )
        copy.start()
        started.append(copy)

    def arrived(dst, ssem, rsem, dev):
        pltpu.make_async_remote_copy(
            src_ref=dst, dst_ref=dst, send_sem=ssem, recv_sem=rsem,
            device_id=dev, device_id_type=MESH,
        ).wait_recv()

    barrier = pltpu.get_barrier_semaphore()
    peers = [zdev(d) for d in (3, -3, 2, -2, 1, -1)]
    peers += [pdev(wrap(yx + j, NP)) for j in range(1, NP)]
    peers.append(sibling)
    loads = [
        pltpu.make_async_copy(src, dst, in_sem.at[i])
        for i, (src, dst) in enumerate(
            ((sampled_hbm, sampled_ref), (centers_hbm, cbuf), (feat_hbm, feat_ref), (label_hbm, label_ref))
        )
    ]
    for load in loads:
        load.start()
    for dev in peers:
        pl.semaphore_signal(barrier, inc=1, device_id=dev, device_id_type=MESH)

    loads[2].wait()
    v = feat_ref[...].astype(jnp.float32)
    fq = lax.rsqrt(jnp.sum(v * v, axis=-1, keepdims=True) + norm_eps)
    xa[yx] = (v * fq).astype(jnp.bfloat16)

    loads[0].wait()
    loads[1].wait()
    owner = z * (2 * NP) + cls
    for b in range(CLS // BLK):
        chosen[b * BLK:(b + 1) * BLK, :] = cbuf[sampled_ref[b, owner]]
    c = chosen[...]
    cq = lax.rsqrt(jnp.sum(c * c, axis=-1, keepdims=True) + norm_eps)
    wa[0, 0] = (c * cq).astype(jnp.bfloat16)

    pl.semaphore_wait(barrier, len(peers))

    sent = 0

    def pass_on(d, e, dev):
        nonlocal sent
        send(wa.at[0, AT[d % NZ]], wa.at[0, AT[(d - e) % NZ]], z_send.at[sent], z_recv.at[(d - e) % NZ], dev)
        sent += 1

    def to_sibling(d):
        p = AT[d % NZ]
        send(wa.at[0, p], wa.at[1, p], s_send.at[p], s_recv.at[p], sibling)

    def class_arrived(d):
        arrived(wa.at[0, AT[d % NZ]], z_send.at[0], z_recv.at[d % NZ], zdev(d))

    for e in (3, -3, 1, -1):
        pass_on(0, e, zdev(e))
    for j in (2, 1, 3):
        send(xa.at[yx], xa.at[yx], a_send.at[j], a_recv.at[SIDE - j], pdev(chip(wrap(first + j, SIDE), second)))
    to_sibling(0)

    loads[3].wait()
    flat = jnp.concatenate([label_ref[pl.ds(z * 12 + i, 1), :] for i in range(12)], axis=1)
    lab = jnp.concatenate(
        [
            jnp.where(core == 0, flat[:, k * 96:k * 96 + 48], flat[:, k * 96 + 48:k * 96 + 96])
            for k in range(NP)
        ],
        axis=1,
    )
    for half in range(2):
        line = yx * 2 + (core if half == 0 else 1 - core)
        for p, d in enumerate(ORDER):
            o = wrap(z + d, NZ) * (2 * NP) + line
            for b in range(2):
                base_ref[half * 32 + p * 2 + b] = (o * BLOCKS + sampled_ref[b, o]) * BLK

    for i in range(SIDE):
        slot = chip(wrap(first + i, SIDE), second)
        if i:
            arrived(xa.at[slot], a_send.at[i], a_recv.at[i], pdev(slot))
        for j in (2, 1, 3):
            send(xa.at[slot], xa.at[slot], b_send.at[j, i], b_recv.at[SIDE - j, i],
                 pdev(chip(first, wrap(second + j, SIDE))))

    for d in (-3, 3):
        class_arrived(d)
        for e in (-d, -d // 3, d // 3):
            pass_on(d, e, zdev(e))
    for d in (1, -1):
        class_arrived(d)
    for d in (-3, 3, 1, -1):
        to_sibling(d)
    for d in (-6, 6):
        class_arrived(d)
        for e in (-d // 6, d // 6):
            pass_on(d, e, zdev(e))
    up = 1 - 2 * core
    far = jnp.where(core == 0, AT[-6 % NZ], AT[6])
    send(wa.at[0, far], wa.at[0, AT[8]], z_send.at[sent], z_recv.at[8], (wrap(z + 2 * up, NZ), cls))
    for d in (-6, 6):
        to_sibling(d)
    for d in (2, -2, 4, -4):
        class_arrived(d)
        to_sibling(d)

    for i in range(SIDE):
        for j in (1, 2, 3):
            slot = chip(wrap(first + i, SIDE), wrap(second + j, SIDE))
            arrived(xa.at[slot], b_send.at[j, i], b_recv.at[j, i], pdev(slot))

    xv = xa[...].reshape(TILE_ROWS, D)
    step = lax.broadcasted_iota(jnp.int32, (BLK, TILE_ROWS), 0)

    def hits(b):
        return (lab - base_ref[b]) == step

    def score(b, carry):
        rows = pl.ds(pl.multiple_of(b * BLK, BLK), BLK)
        hit = hits(b)
        s = logit_scale * et[rows, :] - jnp.where(hit, logit_scale * cosine_margin, 0.0)
        e = jnp.exp(s)
        et[rows, :] = e
        return carry[0] + e, carry[1] + jnp.where(hit, s, 0.0)

    def scores(half, k, carry):
        w = wa[half, k * 8:k * 8 + 8].reshape(256, D)
        q = half * 2 + k
        et[q * 256:(q + 1) * 256, :] = lax.dot_general(
            w, xv, (((1,), (1,)), ((), ())), preferred_element_type=jnp.float32
        )
        return lax.fori_loop(q * 16, q * 16 + 16, score, carry)

    def from_sibling(k):
        for p in range(k * 8, k * 8 + 8):
            arrived(wa.at[1, p], s_send.at[p], s_recv.at[p], sibling)

    zero = jnp.zeros((BLK, TILE_ROWS), jnp.float32)
    sums = scores(0, 0, (zero, zero))
    for d in (5, -5, 7, -7, 8):
        class_arrived(d)
        to_sibling(d)
    from_sibling(0)
    sums = scores(1, 0, sums)
    sums = scores(0, 1, sums)
    from_sibling(1)
    esum, tsum = scores(1, 1, sums)
    tot[0] = jnp.sum(esum, axis=0, keepdims=True)
    tgt[0] = jnp.sum(tsum, axis=0, keepdims=True)
    for j in range(1, NP):
        dev = pdev(wrap(yx + j, NP))
        send(tot.at[0], tot.at[NP - j], t_send.at[j], t_recv.at[NP - j], dev)
    for j in range(1, NP):
        arrived(tot.at[j], t_send.at[j], t_recv.at[j], pdev(wrap(yx + j, NP)))
    total = tot[0]
    for j in range(1, NP):
        total = total + tot[j]
    inverse = 1.0 / total

    def grad(b, carry):
        rows = pl.ds(pl.multiple_of(b * BLK, BLK), BLK)
        hit = hits(b)
        g = (et[rows, :] * inverse - jnp.where(hit, 1.0, 0.0)) * logit_scale
        gt[rows, :] = g.astype(jnp.bfloat16)
        return carry

    def center_part(half, k):
        q = half * 2 + k
        return jnp.dot(gt[q * 256:(q + 1) * 256, :], xv, preferred_element_type=jnp.float32)

    lax.fori_loop(32, 64, grad, 0)
    for k in range(2):
        sib_out[k * 8:k * 8 + 8] = center_part(1, k).astype(jnp.bfloat16).reshape(8, CLS, D)
        send(sib_out.at[pl.ds(k * 8, 8)], sib_in.at[pl.ds(k * 8, 8)], cs_send.at[k], cs_recv.at[k], sibling)
    lax.fori_loop(0, 32, grad, 0)
    for k in range(2):
        p = center_part(0, k).reshape(8, CLS, D)
        arrived(sib_in.at[pl.ds(k * 8, 8)], cs_send.at[k], cs_recv.at[k], sibling)
        p = p + sib_in[k * 8:k * 8 + 8].astype(jnp.float32)
        part[k * 8:k * 8 + 8] = p
        part_b[k * 8:k * 8 + 8] = p.astype(jnp.bfloat16)

    given = 0

    def give(d, dst, rsem, dev):
        nonlocal given
        send(part_b.at[AT[d % NZ]], dst, r_send.at[given], rsem, dev)
        given += 1

    give(8, near8.at[...], r_recv.at[4], (wrap(z - 2 * up, NZ), cls))
    for side, s in ((0, 1), (1, -1)):
        give(-5 * s, near6.at[side, 0], r_recv.at[side * 2], zdev(s))
        give(-7 * s, near6.at[side, 1], r_recv.at[side * 2 + 1], zdev(-s))
    for side, s in ((0, 1), (1, -1)):
        give(-2 * s, near3.at[side, 0], r_recv.at[5 + side * 2], zdev(s))
        give(-4 * s, near3.at[side, 1], r_recv.at[6 + side * 2], zdev(-s))
    for side, s in ((0, 1), (1, -1)):
        give(s, zfin.at[side], q_recv.at[side], zdev(s))

    wv = wa[...].reshape(TILE_CLS, D)
    for k in range(3):
        fval[k * 256:(k + 1) * 256, :] = lax.dot_general(
            gt[:, k * 256:(k + 1) * 256], wv, (((0,), (0,)), ((), ())), preferred_element_type=jnp.float32
        )
    fout[...] = fval[...].astype(jnp.bfloat16).reshape(NP, ROWS, D)
    for i in range(SIDE):
        for j in (2, 1, 3):
            slot = chip(wrap(first + i, SIDE), wrap(second + j, SIDE))
            send(fout.at[slot], fin1.at[SIDE - j, i], f_send.at[j, i], f_recv.at[SIDE - j, i],
                 pdev(chip(first, wrap(second + j, SIDE))))

    for j in range(1, NP):
        send(tgt.at[0], tgt.at[NP - j], u_send.at[j], u_recv.at[NP - j], pdev(wrap(yx + j, NP)))

    arrived(near8.at[...], r_send.at[0], r_recv.at[4], (wrap(z + 2 * up, NZ), cls))
    for side, s in ((0, 1), (1, -1)):
        arrived(near6.at[side, 0], r_send.at[0], r_recv.at[side * 2], zdev(-s))
        arrived(near6.at[side, 1], r_send.at[0], r_recv.at[side * 2 + 1], zdev(s))
        acc = part[AT[-6 * s % NZ]] + near6[side, 0].astype(jnp.float32) + near6[side, 1].astype(jnp.float32)
        acc = acc + jnp.where(core == side, near8[...].astype(jnp.float32), 0.0)
        out6[side] = acc.astype(jnp.bfloat16)
        send(out6.at[side], near3.at[side, 2], q_send.at[side], r_recv.at[9 + side], zdev(-3 * s))

    own_f = None
    for i in (1, 2, 3, 0):
        slot = chip(wrap(first + i, SIDE), second)
        acc = fval[pl.ds(pl.multiple_of(slot * ROWS, 16), ROWS), :]
        for j in (1, 2, 3):
            arrived(fin1.at[j, i], f_send.at[j, i], f_recv.at[j, i], pdev(chip(first, wrap(second + j, SIDE))))
            acc = acc + fin1[j, i].astype(jnp.float32)
        if i:
            fout2[i] = acc.astype(jnp.bfloat16)
            send(fout2.at[i], fin2.at[SIDE - i], h_send.at[i], h_recv.at[SIDE - i], pdev(slot))
        else:
            own_f = acc

    for side, s in ((0, 1), (1, -1)):
        arrived(near3.at[side, 0], r_send.at[0], r_recv.at[5 + side * 2], zdev(-s))
        arrived(near3.at[side, 1], r_send.at[0], r_recv.at[6 + side * 2], zdev(s))
        arrived(near3.at[side, 2], q_send.at[0], r_recv.at[9 + side], zdev(3 * s))
        acc = part[AT[-3 * s % NZ]]
        for i in range(3):
            acc = acc + near3[side, i].astype(jnp.float32)
        out3[side] = acc.astype(jnp.bfloat16)
        send(out3.at[side], zfin.at[2 + side], q_send.at[2 + side], q_recv.at[2 + side], zdev(-3 * s))

    for j in range(1, NP):
        arrived(tgt.at[j], u_send.at[j], u_recv.at[j], pdev(wrap(yx + j, NP)))
    target = tgt[0]
    for j in range(1, NP):
        target = target + tgt[j]
    every = jnp.log(total) - target
    own_loss = every[:, :ROWS]
    for k in range(1, NP):
        own_loss = jnp.where(yx == k, every[:, k * ROWS:(k + 1) * ROWS], own_loss)
    loss_ref[...] = own_loss

    def back(v, q, g):
        return g * q - v * (q * q * q * jnp.sum(v * g, axis=-1, keepdims=True))

    for i in (1, 2, 3):
        arrived(fin2.at[i], h_send.at[i], h_recv.at[i], pdev(chip(wrap(first + i, SIDE), second)))
        own_f = own_f + fin2[i].astype(jnp.float32)
    fgrad_ref[...] = back(v, fq, own_f)

    own_c = part[0]
    for i, d in enumerate((-1, 1, 3, -3)):
        arrived(zfin.at[i], q_send.at[0], q_recv.at[i], zdev(d))
        own_c = own_c + zfin[i].astype(jnp.float32)
    cgrad_ref[...] = back(c, cq, own_c)

    for copy in started:
        copy.wait_send()


def hand_over(a_ref, b_ref, c_ref, a_out, b_out, c_out):
    a_out[...] = a_ref[...]
    b_out[...] = b_ref[...]
    c_out[...] = c_ref[...]


def scratch():
    bf, f32, dma = jnp.bfloat16, jnp.float32, pltpu.SemaphoreType.DMA
    vm = pltpu.VMEM
    return [
        vm((ROWS, D), bf), vm((BLOCKS, BLK, D), f32), vm((192, 128), jnp.int32),
        pltpu.SMEM((2, 2 * NZ * NP), jnp.int32), pltpu.SMEM((64,), jnp.int32),
        vm((CLS, D), f32), vm((NP, ROWS, D), bf), vm((2, NZ, CLS, D), bf),
        vm((TILE_CLS, TILE_ROWS), f32), vm((TILE_CLS, TILE_ROWS), bf),
        vm((NP, 1, TILE_ROWS), f32), vm((NP, 1, TILE_ROWS), f32),
        vm((NZ, CLS, D), bf), vm((NZ, CLS, D), bf), vm((NZ, CLS, D), f32), vm((NZ, CLS, D), bf),
        vm((2, 2, CLS, D), bf), vm((CLS, D), bf), vm((2, 3, CLS, D), bf),
        vm((2, CLS, D), bf), vm((2, CLS, D), bf), vm((4, CLS, D), bf),
        vm((TILE_ROWS, D), f32), vm((NP, ROWS, D), bf), vm((SIDE, SIDE, ROWS, D), bf),
        vm((SIDE, ROWS, D), bf), vm((SIDE, ROWS, D), bf),
        dma((4,)), dma((NZ,)), dma((NZ,)), dma((NZ,)), dma((NZ,)), dma((SIDE,)), dma((SIDE,)),
        dma((SIDE, SIDE)), dma((SIDE, SIDE)),
        dma((NP,)), dma((NP,)), dma((NP,)), dma((NP,)), dma((2,)), dma((2,)),
        dma((11,)), dma((11,)), dma((4,)), dma((4,)), dma((SIDE, SIDE)), dma((SIDE, SIDE)), dma((SIDE,)), dma((SIDE,)),
    ]


def local(features, centers, labels, sampled):
    hbm = pl.BlockSpec(memory_space=pltpu.HBM)
    vmem = pl.BlockSpec(memory_space=pltpu.VMEM)
    losses, feature_grad, center_grad = pl.pallas_call(
        kernel,
        out_shape=(
            jax.ShapeDtypeStruct((1, ROWS), jnp.float32),
            jax.ShapeDtypeStruct((ROWS, D), jnp.float32),
            jax.ShapeDtypeStruct((CLS, D), jnp.float32),
        ),
        in_specs=[hbm, hbm, hbm, hbm],
        out_specs=(vmem, vmem, vmem),
        scratch_shapes=scratch(),
        compiler_params=pltpu.CompilerParams(
            collective_id=0, has_side_effects=True, vmem_limit_bytes=62 * 1024 * 1024
        ),
        name="margin_step",
    )(features, centers.reshape(BLOCKS, BLK, D), labels.reshape(192, 128), sampled.T)
    losses, feature_grad, center_grad = pl.pallas_call(
        hand_over,
        out_shape=(
            jax.ShapeDtypeStruct((1, ROWS), jnp.float32),
            jax.ShapeDtypeStruct((ROWS, D), jnp.float32),
            jax.ShapeDtypeStruct((CLS, D), jnp.float32),
        ),
        in_specs=[vmem] * 3,
        out_specs=(vmem,) * 3,
        compiler_params=pltpu.CompilerParams(vmem_limit_bytes=62 * 1024 * 1024),
        name="hand_over",
    )(losses, feature_grad, center_grad)
    return (losses.reshape(ROWS), feature_grad, center_grad)


def solution(mesh):
    placed = (P(("dp", "cls"), None), P(("dp", "cls"), None), P(), P())
    return jax.shard_map(
        local,
        mesh=mesh,
        in_specs=placed,
        out_specs=(P(("dp", "cls")), P(("dp", "cls"), None), P(("dp", "cls"), None)),
        check_vma=False,
    )
```

```python
import functools

import jax
import jax.numpy as jnp
from jax import lax
from jax.experimental import pallas as pl
from jax.experimental.pallas import tpu as pltpu
from jax.sharding import PartitionSpec as P

MESH = pl.DeviceIdType.MESH
BLK = 16
D = 512
ROWS = 48
CLS = 32
NZ = 16
NP = 16
SIDE = 4
BLOCKS = 128
TILE_ROWS = NP * ROWS
TILE_CLS = 2 * NZ * CLS

logit_scale = 64.0
cosine_margin = 0.35
norm_eps = 1e-06

ORDER = (0, 1, -1, 3, -3, 2, -2, 6, -6, 4, -4, 5, -5, 7, -7, 8)
AT = {d % NZ: p for p, d in enumerate(ORDER)}


def wrap(value, size):
    return lax.rem(value + size, size)


def kernel(
    feat_hbm, centers_hbm, label_hbm, sampled_hbm,
    loss_ref, fgrad_ref, cgrad_ref,
    feat_ref, cbuf, label_ref, sampled_ref, base_ref, chosen, xa, wa, et, gt, labcol, sn, en, hn, tot, tgt,
    sib_out, sib_in, part, part_b, near6, near8, near3, out6, out3, zfin,
    fval, hval, fout, fin1, fout2, fin2,
    in_sem, z_send, z_recv, s_send, s_recv, a_send, a_recv, b_send, b_recv,
    t_send, t_recv, u_send, u_recv, cs_send, cs_recv,
    r_send, r_recv, q_send, q_recv, f_send, f_recv, h_send, h_recv,
):
    z = lax.axis_index("dp")
    cls = lax.axis_index("cls")
    core = lax.rem(cls, 2)
    yx = lax.div(cls, 2)
    y = lax.div(yx, SIDE)
    x = lax.rem(yx, SIDE)
    first = jnp.where(core == 0, y, x)
    second = jnp.where(core == 0, x, y)

    def chip(p1, p2):
        return jnp.where(core == 0, p1 * SIDE + p2, p2 * SIDE + p1)

    def zdev(d):
        return (wrap(z + d, NZ), cls)

    def pdev(slot):
        return (z, slot * 2 + core)

    sibling = (z, yx * 2 + 1 - core)
    started = []

    def send(src, dst, ssem, rsem, dev):
        copy = pltpu.make_async_remote_copy(
            src_ref=src, dst_ref=dst, send_sem=ssem, recv_sem=rsem,
            device_id=dev, device_id_type=MESH,
        )
        copy.start()
        started.append(copy)

    def arrived(dst, ssem, rsem, dev):
        pltpu.make_async_remote_copy(
            src_ref=dst, dst_ref=dst, send_sem=ssem, recv_sem=rsem,
            device_id=dev, device_id_type=MESH,
        ).wait_recv()

    barrier = pltpu.get_barrier_semaphore()
    peers = [zdev(d) for d in (3, -3, 2, -2, 1, -1)]
    peers += [pdev(chip(wrap(first + j, SIDE), second)) for j in (2, 1, 3)]
    peers += [pdev(chip(first, wrap(second + j, SIDE))) for j in (2, 1, 3)]
    peers.append(sibling)
    loads = [
        pltpu.make_async_copy(src, dst, in_sem.at[i])
        for i, (src, dst) in enumerate(
            [(sampled_hbm, sampled_ref)]
            + [(centers_hbm.at[pl.ds(k * 32, 32)], cbuf.at[pl.ds(k * 32, 32)]) for k in range(4)]
            + [(feat_hbm, feat_ref), (label_hbm, label_ref)]
        )
    ]
    for load in loads:
        load.start()
    for dev in peers:
        pl.semaphore_signal(barrier, inc=1, device_id=dev, device_id_type=MESH)

    loads[5].wait()
    v = feat_ref[...].astype(jnp.float32)
    fq = lax.rsqrt(jnp.sum(v * v, axis=-1, keepdims=True) + norm_eps)
    xa[yx] = (v * fq).astype(jnp.bfloat16)

    for load in loads[:5]:
        load.wait()
    owner = z * (2 * NP) + cls
    for b in range(CLS // BLK):
        chosen[b * BLK:(b + 1) * BLK, :] = cbuf[sampled_ref[b, owner]]
    c = chosen[...]
    cq = lax.rsqrt(jnp.sum(c * c, axis=-1, keepdims=True) + norm_eps)
    wa[0, 0] = (c * cq).astype(jnp.bfloat16)

    pl.semaphore_wait(barrier, len(peers))

    sent = 0

    def pass_on(d, e, dev):
        nonlocal sent
        send(wa.at[0, AT[d % NZ]], wa.at[0, AT[(d - e) % NZ]], z_send.at[sent], z_recv.at[(d - e) % NZ], dev)
        sent += 1

    def to_sibling(d):
        p = AT[d % NZ]
        send(wa.at[0, p], wa.at[1, p], s_send.at[p], s_recv.at[p], sibling)

    def class_arrived(d):
        arrived(wa.at[0, AT[d % NZ]], z_send.at[0], z_recv.at[d % NZ], zdev(d))

    for e in (3, -3, 1, -1):
        pass_on(0, e, zdev(e))
    for j in (2, 1, 3):
        send(xa.at[yx], xa.at[yx], a_send.at[j], a_recv.at[SIDE - j], pdev(chip(wrap(first + j, SIDE), second)))
    to_sibling(0)

    loads[6].wait()
    flat = jnp.concatenate([label_ref[pl.ds(z * 12 + i, 1), :] for i in range(12)], axis=1)
    lab = jnp.concatenate(
        [
            jnp.where(core == 0, flat[:, k * 96:k * 96 + 48], flat[:, k * 96 + 48:k * 96 + 96])
            for k in range(NP)
        ],
        axis=1,
    )
    labcol[...] = jnp.transpose(jnp.broadcast_to(lab, (128, TILE_ROWS)))
    for half in range(2):
        line = yx * 2 + (core if half == 0 else 1 - core)
        for p, d in enumerate(ORDER):
            o = wrap(z + d, NZ) * (2 * NP) + line
            for b in range(2):
                base_ref[half * 32 + p * 2 + b] = (o * BLOCKS + sampled_ref[b, o]) * BLK

    for i in range(SIDE):
        slot = chip(wrap(first + i, SIDE), second)
        if i:
            arrived(xa.at[slot], a_send.at[i], a_recv.at[i], pdev(slot))
        for j in (2, 1, 3):
            send(xa.at[slot], xa.at[slot], b_send.at[j, i], b_recv.at[SIDE - j, i],
                 pdev(chip(first, wrap(second + j, SIDE))))

    for d in (-3, 3):
        class_arrived(d)
        for e in (-d, -d // 3, d // 3):
            pass_on(d, e, zdev(e))
    for d in (1, -1):
        class_arrived(d)
    for d in (1, -1, 3, -3):
        to_sibling(d)
    for d in (-6, 6):
        class_arrived(d)
    up = 1 - 2 * core
    far = jnp.where(core == 0, AT[-6 % NZ], AT[6])
    send(wa.at[0, far], wa.at[0, AT[8]], z_send.at[sent], z_recv.at[8], (wrap(z + 2 * up, NZ), cls))
    sent += 1
    for d in (-6, 6):
        for e in (-d // 6, d // 6):
            pass_on(d, e, zdev(e))
    for d in (2, -2, 4, -4):
        class_arrived(d)
        to_sibling(d)
    for d in (-6, 6):
        to_sibling(d)

    for i in range(SIDE):
        for j in (1, 2, 3):
            slot = chip(wrap(first + i, SIDE), wrap(second + j, SIDE))
            arrived(xa.at[slot], b_send.at[j, i], b_recv.at[j, i], pdev(slot))

    xv = xa[...].reshape(TILE_ROWS, D)
    step = lax.broadcasted_iota(jnp.int32, (BLK, TILE_ROWS), 0)

    def hits(b):
        return (lab - base_ref[b]) == step

    def score(b, carry):
        rows = pl.ds(pl.multiple_of(b * BLK, BLK), BLK)
        hit = hits(b)
        s = logit_scale * et[rows, :] - jnp.where(hit, logit_scale * cosine_margin, 0.0)
        e = jnp.exp(s)
        et[rows, :] = e
        return carry[0] + e, carry[1] + jnp.where(hit, s, 0.0)

    def scores(half, k, carry):
        w = wa[half, k * 8:k * 8 + 8].reshape(256, D)
        q = half * 2 + k
        et[q * 256:(q + 1) * 256, :] = lax.dot_general(
            w, xv, (((1,), (1,)), ((), ())), preferred_element_type=jnp.float32
        )
        return lax.fori_loop(q * 16, q * 16 + 16, score, carry)

    def from_sibling(k):
        for p in range(k * 8, k * 8 + 8):
            arrived(wa.at[1, p], s_send.at[p], s_recv.at[p], sibling)

    lane = lax.broadcasted_iota(jnp.int32, (1, 128), 1)

    def ids(at):
        row = lax.rem(lane, BLK) + base_ref[at]
        for j in range(1, 8):
            row = jnp.where(lax.div(lane, BLK) == j, lax.rem(lane, BLK) + base_ref[at + j], row)
        return row

    def feature_part(k):
        w = wa[:, k * 8:k * 8 + 8].reshape(512, D)
        classes = [ids(half * 32 + k * 16 + j * 8) for half in range(2) for j in range(2)]
        for i in range(3):
            rows = slice(i * 256, (i + 1) * 256)
            sn[...] = lax.dot_general(xv[rows, :], w, (((1,), (1,)), ((), ())), preferred_element_type=jnp.float32)
            for g in range(4):
                cols = slice(g * 128, (g + 1) * 128)
                hit = labcol[rows, :] == classes[g]
                e = jnp.exp(logit_scale * sn[:, cols] - jnp.where(hit, logit_scale * cosine_margin, 0.0))
                en[:, cols] = e.astype(jnp.bfloat16)
                hn[:, cols] = jnp.where(hit, 1.0, 0.0).astype(jnp.bfloat16)
            for ref, lhs in ((fval, en), (hval, hn)):
                more = jnp.dot(lhs[...], w, preferred_element_type=jnp.float32)
                ref[rows, :] = more if k == 0 else ref[rows, :] + more

    zero = jnp.zeros((BLK, TILE_ROWS), jnp.float32)
    sums = scores(0, 0, (zero, zero))
    from_sibling(0)
    sums = scores(1, 0, sums)
    feature_part(0)
    for d in (5, -5, 7, -7, 8):
        class_arrived(d)
        to_sibling(d)
    sums = scores(0, 1, sums)
    from_sibling(1)
    esum, tsum = scores(1, 1, sums)
    tot[0] = jnp.sum(esum, axis=0, keepdims=True)
    tgt[0] = jnp.sum(tsum, axis=0, keepdims=True)
    for j in range(1, NP):
        dev = pdev(wrap(yx + j, NP))
        send(tot.at[0], tot.at[NP - j], t_send.at[j], t_recv.at[NP - j], dev)

    feature_part(1)

    for j in range(1, NP):
        arrived(tot.at[j], t_send.at[j], t_recv.at[j], pdev(wrap(yx + j, NP)))
    total = tot[0]
    for j in range(1, NP):
        total = total + tot[j]
    inverse = 1.0 / total

    def grad(b, carry):
        rows = pl.ds(pl.multiple_of(b * BLK, BLK), BLK)
        hit = hits(b)
        g = (et[rows, :] * inverse - jnp.where(hit, 1.0, 0.0)) * logit_scale
        gt[rows, :] = g.astype(jnp.bfloat16)
        return carry

    def center_part(half, k):
        q = half * 2 + k
        return jnp.dot(gt[q * 256:(q + 1) * 256, :], xv, preferred_element_type=jnp.float32)

    given = 0

    def give(d, dst, rsem, dev):
        nonlocal given
        send(part_b.at[AT[d % NZ]], dst, r_send.at[given], rsem, dev)
        given += 1

    def other_part(k):
        lax.fori_loop(32 + k * 16, 48 + k * 16, grad, 0)
        sib_out[k * 8:k * 8 + 8] = center_part(1, k).astype(jnp.bfloat16).reshape(8, CLS, D)
        send(sib_out.at[pl.ds(k * 8, 8)], sib_in.at[pl.ds(k * 8, 8)], cs_send.at[k], cs_recv.at[k], sibling)

    def own_part(k):
        lax.fori_loop(k * 16, k * 16 + 16, grad, 0)
        part[k * 8:k * 8 + 8] = center_part(0, k).reshape(8, CLS, D)

    def add_up(k):
        arrived(sib_in.at[pl.ds(k * 8, 8)], cs_send.at[k], cs_recv.at[k], sibling)
        p = part[k * 8:k * 8 + 8] + sib_in[k * 8:k * 8 + 8].astype(jnp.float32)
        part[k * 8:k * 8 + 8] = p
        part_b[k * 8:k * 8 + 8] = p.astype(jnp.bfloat16)

    other_part(1)
    own_part(1)
    other_part(0)
    add_up(1)
    give(8, near8.at[...], r_recv.at[4], (wrap(z - 2 * up, NZ), cls))
    for side, s in ((0, 1), (1, -1)):
        give(-7 * s, near6.at[side, 1], r_recv.at[side * 2 + 1], zdev(-s))
        give(-5 * s, near6.at[side, 0], r_recv.at[side * 2], zdev(s))
    for side, s in ((0, 1), (1, -1)):
        give(-4 * s, near3.at[side, 1], r_recv.at[6 + side * 2], zdev(-s))

    column = jnp.transpose(jnp.broadcast_to(inverse, (8, TILE_ROWS)))[:, :1]
    fsum = (fval[...] * column - hval[...]) * logit_scale
    fval[...] = fsum
    fout[...] = fsum.astype(jnp.bfloat16).reshape(NP, ROWS, D)
    for i in (1, 2, 3, 0):
        for j in (2, 1, 3):
            slot = chip(wrap(first + i, SIDE), wrap(second + j, SIDE))
            send(fout.at[slot], fin1.at[SIDE - j, i], f_send.at[j, i], f_recv.at[SIDE - j, i],
                 pdev(chip(first, wrap(second + j, SIDE))))

    own_part(0)
    add_up(0)
    for side, s in ((0, 1), (1, -1)):
        give(-2 * s, near3.at[side, 0], r_recv.at[5 + side * 2], zdev(s))
    for side, s in ((0, 1), (1, -1)):
        give(s, zfin.at[side], q_recv.at[side], zdev(s))
    for j in range(1, NP):
        send(tgt.at[0], tgt.at[NP - j], u_send.at[j], u_recv.at[NP - j], pdev(wrap(yx + j, NP)))

    arrived(near8.at[...], r_send.at[0], r_recv.at[4], (wrap(z + 2 * up, NZ), cls))
    for side, s in ((0, 1), (1, -1)):
        arrived(near6.at[side, 0], r_send.at[0], r_recv.at[side * 2], zdev(-s))
        arrived(near6.at[side, 1], r_send.at[0], r_recv.at[side * 2 + 1], zdev(s))
        acc = part[AT[-6 * s % NZ]] + near6[side, 0].astype(jnp.float32) + near6[side, 1].astype(jnp.float32)
        acc = acc + jnp.where(core == side, near8[...].astype(jnp.float32), 0.0)
        out6[side] = acc.astype(jnp.bfloat16)
        send(out6.at[side], zfin.at[4 + side], q_send.at[side], q_recv.at[4 + side], zdev(-6 * s))

    for side, s in ((0, 1), (1, -1)):
        arrived(near3.at[side, 0], r_send.at[0], r_recv.at[5 + side * 2], zdev(-s))
        arrived(near3.at[side, 1], r_send.at[0], r_recv.at[6 + side * 2], zdev(s))
        acc = part[AT[-3 * s % NZ]] + near3[side, 0].astype(jnp.float32) + near3[side, 1].astype(jnp.float32)
        out3[side] = acc.astype(jnp.bfloat16)
        send(out3.at[side], zfin.at[2 + side], q_send.at[2 + side], q_recv.at[2 + side], zdev(-3 * s))

    own_f = None
    for i in (1, 2, 3, 0):
        slot = chip(wrap(first + i, SIDE), second)
        acc = fval[pl.ds(pl.multiple_of(slot * ROWS, 16), ROWS), :]
        for j in (1, 2, 3):
            arrived(fin1.at[j, i], f_send.at[j, i], f_recv.at[j, i], pdev(chip(first, wrap(second + j, SIDE))))
            acc = acc + fin1[j, i].astype(jnp.float32)
        if i:
            fout2[i] = acc.astype(jnp.bfloat16)
            send(fout2.at[i], fin2.at[SIDE - i], h_send.at[i], h_recv.at[SIDE - i], pdev(slot))
        else:
            own_f = acc

    for j in range(1, NP):
        arrived(tgt.at[j], u_send.at[j], u_recv.at[j], pdev(wrap(yx + j, NP)))
    target = tgt[0]
    for j in range(1, NP):
        target = target + tgt[j]
    every = jnp.log(total) - target
    own_loss = every[:, :ROWS]
    for k in range(1, NP):
        own_loss = jnp.where(yx == k, every[:, k * ROWS:(k + 1) * ROWS], own_loss)
    loss_ref[...] = own_loss

    def back(v, q, g):
        return g * q - v * (q * q * q * jnp.sum(v * g, axis=-1, keepdims=True))

    for i in (1, 2, 3):
        arrived(fin2.at[i], h_send.at[i], h_recv.at[i], pdev(chip(wrap(first + i, SIDE), second)))
        own_f = own_f + fin2[i].astype(jnp.float32)
    fgrad_ref[...] = back(v, fq, own_f)

    own_c = part[0]
    for i, d in enumerate((-1, 1, 3, -3, 6, -6)):
        arrived(zfin.at[i], q_send.at[0], q_recv.at[i], zdev(d))
        own_c = own_c + zfin[i].astype(jnp.float32)
    cgrad_ref[...] = back(c, cq, own_c)

    for copy in started:
        copy.wait_send()


def hand_over(a_ref, b_ref, c_ref, a_out, b_out, c_out):
    a_out[...] = a_ref[...]
    b_out[...] = b_ref[...]
    c_out[...] = c_ref[...]


def scratch():
    bf, f32, dma = jnp.bfloat16, jnp.float32, pltpu.SemaphoreType.DMA
    vm = pltpu.VMEM
    return [
        vm((ROWS, D), bf), vm((BLOCKS, BLK, D), f32), vm((192, 128), jnp.int32),
        pltpu.SMEM((2, 2 * NZ * NP), jnp.int32), pltpu.SMEM((64,), jnp.int32),
        vm((CLS, D), f32), vm((NP, ROWS, D), bf), vm((2, NZ, CLS, D), bf),
        vm((TILE_CLS, TILE_ROWS), f32), vm((TILE_CLS, TILE_ROWS), bf), vm((TILE_ROWS, 128), jnp.int32),
        vm((256, 512), f32), vm((256, 512), bf), vm((256, 512), bf),
        vm((NP, 1, TILE_ROWS), f32), vm((NP, 1, TILE_ROWS), f32),
        vm((NZ, CLS, D), bf), vm((NZ, CLS, D), bf), vm((NZ, CLS, D), f32), vm((NZ, CLS, D), bf),
        vm((2, 2, CLS, D), bf), vm((CLS, D), bf), vm((2, 2, CLS, D), bf),
        vm((2, CLS, D), bf), vm((2, CLS, D), bf), vm((6, CLS, D), bf),
        vm((TILE_ROWS, D), f32), vm((TILE_ROWS, D), f32), vm((NP, ROWS, D), bf), vm((SIDE, SIDE, ROWS, D), bf),
        vm((SIDE, ROWS, D), bf), vm((SIDE, ROWS, D), bf),
        dma((7,)), dma((NZ,)), dma((NZ,)), dma((NZ,)), dma((NZ,)), dma((SIDE,)), dma((SIDE,)),
        dma((SIDE, SIDE)), dma((SIDE, SIDE)),
        dma((NP,)), dma((NP,)), dma((NP,)), dma((NP,)), dma((2,)), dma((2,)),
        dma((11,)), dma((9,)), dma((4,)), dma((6,)), dma((SIDE, SIDE)), dma((SIDE, SIDE)), dma((SIDE,)), dma((SIDE,)),
    ]


def local(features, centers, labels, sampled):
    hbm = pl.BlockSpec(memory_space=pltpu.HBM)
    vmem = pl.BlockSpec(memory_space=pltpu.VMEM)
    losses, feature_grad, center_grad = pl.pallas_call(
        kernel,
        out_shape=(
            jax.ShapeDtypeStruct((1, ROWS), jnp.float32),
            jax.ShapeDtypeStruct((ROWS, D), jnp.float32),
            jax.ShapeDtypeStruct((CLS, D), jnp.float32),
        ),
        in_specs=[hbm, hbm, hbm, hbm],
        out_specs=(vmem, vmem, vmem),
        scratch_shapes=scratch(),
        compiler_params=pltpu.CompilerParams(
            collective_id=0, has_side_effects=True, vmem_limit_bytes=62 * 1024 * 1024
        ),
        name="margin_step",
    )(features, centers.reshape(BLOCKS, BLK, D), labels.reshape(192, 128), sampled.T)
    losses, feature_grad, center_grad = pl.pallas_call(
        hand_over,
        out_shape=(
            jax.ShapeDtypeStruct((1, ROWS), jnp.float32),
            jax.ShapeDtypeStruct((ROWS, D), jnp.float32),
            jax.ShapeDtypeStruct((CLS, D), jnp.float32),
        ),
        in_specs=[vmem] * 3,
        out_specs=(vmem,) * 3,
        compiler_params=pltpu.CompilerParams(vmem_limit_bytes=62 * 1024 * 1024),
        name="hand_over",
    )(losses, feature_grad, center_grad)
    return (losses.reshape(ROWS), feature_grad, center_grad)


def solution(mesh):
    placed = (P(("dp", "cls"), None), P(("dp", "cls"), None), P(), P())
    return jax.shard_map(
        local,
        mesh=mesh,
        in_specs=placed,
        out_specs=(P(("dp", "cls")), P(("dp", "cls"), None), P(("dp", "cls"), None)),
        check_vma=False,
    )
```

```python
import functools

import jax
import jax.numpy as jnp
from jax import lax
from jax.experimental import pallas as pl
from jax.experimental.pallas import tpu as pltpu
from jax.sharding import PartitionSpec as P

MESH = pl.DeviceIdType.MESH
BLK = 16
D = 512
ROWS = 48
CLS = 32
NZ = 16
NP = 16
SIDE = 4
BLOCKS = 128
TILE_ROWS = NP * ROWS
TILE_CLS = 2 * NZ * CLS

logit_scale = 64.0
cosine_margin = 0.35
norm_eps = 1e-06

ORDER = (0, 1, -1, 3, -3, 2, -2, 6, -6, 4, -4, 5, -5, 7, -7, 8)
AT = {d % NZ: p for p, d in enumerate(ORDER)}


def wrap(value, size):
    return lax.rem(value + size, size)


def kernel(
    feat_hbm, centers_hbm, label_hbm, sampled_hbm,
    loss_ref, fgrad_ref, cgrad_ref,
    feat_ref, cbuf, label_ref, sampled_ref, base_ref, chosen, xa, wa, et, gt, labcol, sn, en, hn, tot, tgt,
    sib_out, sib_in, part, part_b, near6, near8, near3, out6, out3, zfin,
    fval, hval, fout, fin1, fout2, fin2,
    in_sem, z_send, z_recv, s_send, s_recv, a_send, a_recv, b_send, b_recv,
    t_send, t_recv, u_send, u_recv, cs_send, cs_recv,
    r_send, r_recv, q_send, q_recv, f_send, f_recv, h_send, h_recv,
):
    z = lax.axis_index("dp")
    cls = lax.axis_index("cls")
    core = lax.rem(cls, 2)
    yx = lax.div(cls, 2)
    y = lax.div(yx, SIDE)
    x = lax.rem(yx, SIDE)
    first = jnp.where(core == 0, y, x)
    second = jnp.where(core == 0, x, y)

    def chip(p1, p2):
        return jnp.where(core == 0, p1 * SIDE + p2, p2 * SIDE + p1)

    def zdev(d):
        return (wrap(z + d, NZ), cls)

    def pdev(slot):
        return (z, slot * 2 + core)

    sibling = (z, yx * 2 + 1 - core)
    started = []

    def send(src, dst, ssem, rsem, dev):
        copy = pltpu.make_async_remote_copy(
            src_ref=src, dst_ref=dst, send_sem=ssem, recv_sem=rsem,
            device_id=dev, device_id_type=MESH,
        )
        copy.start()
        started.append(copy)

    def arrived(dst, ssem, rsem, dev):
        pltpu.make_async_remote_copy(
            src_ref=dst, dst_ref=dst, send_sem=ssem, recv_sem=rsem,
            device_id=dev, device_id_type=MESH,
        ).wait_recv()

    barrier = pltpu.get_barrier_semaphore()
    peers = [zdev(d) for d in (3, -3, 2, -2, 1, -1)]
    peers += [pdev(chip(wrap(first + j, SIDE), second)) for j in (2, 1, 3)]
    peers += [pdev(chip(first, wrap(second + j, SIDE))) for j in (2, 1, 3)]
    peers.append(sibling)
    loads = [
        pltpu.make_async_copy(src, dst, in_sem.at[i])
        for i, (src, dst) in enumerate(
            [(sampled_hbm, sampled_ref)]
            + [(centers_hbm.at[pl.ds(k * 32, 32)], cbuf.at[pl.ds(k * 32, 32)]) for k in range(4)]
            + [(feat_hbm, feat_ref), (label_hbm, label_ref)]
        )
    ]
    for load in loads:
        load.start()
    for dev in peers:
        pl.semaphore_signal(barrier, inc=1, device_id=dev, device_id_type=MESH)

    loads[5].wait()
    v = feat_ref[...].astype(jnp.float32)
    fq = lax.rsqrt(jnp.sum(v * v, axis=-1, keepdims=True) + norm_eps)
    xa[yx] = (v * fq).astype(jnp.bfloat16)

    for load in loads[:5]:
        load.wait()
    owner = z * (2 * NP) + cls
    for b in range(CLS // BLK):
        chosen[b * BLK:(b + 1) * BLK, :] = cbuf[sampled_ref[b, owner]]
    c = chosen[...]
    cq = lax.rsqrt(jnp.sum(c * c, axis=-1, keepdims=True) + norm_eps)
    wa[0, 0] = (c * cq).astype(jnp.bfloat16)

    pl.semaphore_wait(barrier, len(peers))

    sent = 0

    def pass_on(d, e, dev):
        nonlocal sent
        send(wa.at[0, AT[d % NZ]], wa.at[0, AT[(d - e) % NZ]], z_send.at[sent], z_recv.at[(d - e) % NZ], dev)
        sent += 1

    def to_sibling(d):
        p = AT[d % NZ]
        send(wa.at[0, p], wa.at[1, p], s_send.at[p], s_recv.at[p], sibling)

    def class_arrived(d):
        arrived(wa.at[0, AT[d % NZ]], z_send.at[0], z_recv.at[d % NZ], zdev(d))

    for e in (3, -3, 1, -1):
        pass_on(0, e, zdev(e))
    for j in (2, 1, 3):
        send(xa.at[yx], xa.at[yx], a_send.at[j], a_recv.at[SIDE - j], pdev(chip(wrap(first + j, SIDE), second)))
    to_sibling(0)

    loads[6].wait()
    flat = jnp.concatenate([label_ref[pl.ds(z * 12 + i, 1), :] for i in range(12)], axis=1)
    lab = jnp.concatenate(
        [
            jnp.where(core == 0, flat[:, k * 96:k * 96 + 48], flat[:, k * 96 + 48:k * 96 + 96])
            for k in range(NP)
        ],
        axis=1,
    )
    labcol[...] = jnp.transpose(jnp.broadcast_to(lab, (128, TILE_ROWS)))
    for half in range(2):
        line = yx * 2 + (core if half == 0 else 1 - core)
        for p, d in enumerate(ORDER):
            o = wrap(z + d, NZ) * (2 * NP) + line
            for b in range(2):
                base_ref[half * 32 + p * 2 + b] = (o * BLOCKS + sampled_ref[b, o]) * BLK

    for i in range(SIDE):
        slot = chip(wrap(first + i, SIDE), second)
        if i:
            arrived(xa.at[slot], a_send.at[i], a_recv.at[i], pdev(slot))
        for j in (2, 1, 3):
            send(xa.at[slot], xa.at[slot], b_send.at[j, i], b_recv.at[SIDE - j, i],
                 pdev(chip(first, wrap(second + j, SIDE))))

    for d in (-3, 3):
        class_arrived(d)
        for e in (-d, -d // 3, d // 3):
            pass_on(d, e, zdev(e))
    for d in (1, -1):
        class_arrived(d)
    for d in (1, -1, 3, -3):
        to_sibling(d)
    for d in (-6, 6):
        class_arrived(d)
    up = 1 - 2 * core
    far = jnp.where(core == 0, AT[-6 % NZ], AT[6])
    send(wa.at[0, far], wa.at[0, AT[8]], z_send.at[sent], z_recv.at[8], (wrap(z + 2 * up, NZ), cls))
    sent += 1
    for d in (-6, 6):
        for e in (-d // 6, d // 6):
            pass_on(d, e, zdev(e))
    for d in (2, -2, 4, -4):
        class_arrived(d)
        to_sibling(d)
    for d in (-6, 6):
        to_sibling(d)

    for i in range(SIDE):
        for j in (1, 2, 3):
            slot = chip(wrap(first + i, SIDE), wrap(second + j, SIDE))
            arrived(xa.at[slot], b_send.at[j, i], b_recv.at[j, i], pdev(slot))

    xv = xa[...].reshape(TILE_ROWS, D)
    step = lax.broadcasted_iota(jnp.int32, (BLK, TILE_ROWS), 0)

    def hits(b):
        return (lab - base_ref[b]) == step

    def score(b, carry):
        rows = pl.ds(pl.multiple_of(b * BLK, BLK), BLK)
        hit = hits(b)
        s = logit_scale * et[rows, :] - jnp.where(hit, logit_scale * cosine_margin, 0.0)
        e = jnp.exp(s)
        et[rows, :] = e
        return carry[0] + e, carry[1] + jnp.where(hit, s, 0.0)

    def scores(half, k, carry):
        w = wa[half, k * 8:k * 8 + 8].reshape(256, D)
        q = half * 2 + k
        et[q * 256:(q + 1) * 256, :] = lax.dot_general(
            w, xv, (((1,), (1,)), ((), ())), preferred_element_type=jnp.float32
        )
        return lax.fori_loop(q * 16, q * 16 + 16, score, carry)

    def from_sibling(k):
        for p in range(k * 8, k * 8 + 8):
            arrived(wa.at[1, p], s_send.at[p], s_recv.at[p], sibling)

    lane = lax.broadcasted_iota(jnp.int32, (1, 128), 1)

    def ids(at):
        row = lax.rem(lane, BLK) + base_ref[at]
        for j in range(1, 8):
            row = jnp.where(lax.div(lane, BLK) == j, lax.rem(lane, BLK) + base_ref[at + j], row)
        return row

    def feature_part(k):
        w = wa[:, k * 8:k * 8 + 8].reshape(512, D)
        classes = [ids(half * 32 + k * 16 + j * 8) for half in range(2) for j in range(2)]
        for i in range(3):
            rows = slice(i * 256, (i + 1) * 256)
            sn[...] = lax.dot_general(xv[rows, :], w, (((1,), (1,)), ((), ())), preferred_element_type=jnp.float32)
            for g in range(4):
                cols = slice(g * 128, (g + 1) * 128)
                hit = labcol[rows, :] == classes[g]
                e = jnp.exp(logit_scale * sn[:, cols] - jnp.where(hit, logit_scale * cosine_margin, 0.0))
                en[:, cols] = e.astype(jnp.bfloat16)
                hn[:, cols] = jnp.where(hit, 1.0, 0.0).astype(jnp.bfloat16)
            for ref, lhs in ((fval, en), (hval, hn)):
                more = jnp.dot(lhs[...], w, preferred_element_type=jnp.float32)
                ref[rows, :] = more if k == 0 else ref[rows, :] + more

    zero = jnp.zeros((BLK, TILE_ROWS), jnp.float32)
    sums = scores(0, 0, (zero, zero))
    from_sibling(0)
    sums = scores(1, 0, sums)
    feature_part(0)
    for d in (5, -5, 7, -7, 8):
        class_arrived(d)
        to_sibling(d)
    sums = scores(0, 1, sums)
    from_sibling(1)
    esum, tsum = scores(1, 1, sums)
    tot[0] = jnp.sum(esum, axis=0, keepdims=True)
    tgt[0] = jnp.sum(tsum, axis=0, keepdims=True)
    for j in range(1, NP):
        dev = pdev(wrap(yx + j, NP))
        send(tot.at[0], tot.at[NP - j], t_send.at[j], t_recv.at[NP - j], dev)

    feature_part(1)

    for j in range(1, NP):
        arrived(tot.at[j], t_send.at[j], t_recv.at[j], pdev(wrap(yx + j, NP)))
    total = tot[0]
    for j in range(1, NP):
        total = total + tot[j]
    inverse = 1.0 / total

    def grad(b, carry):
        rows = pl.ds(pl.multiple_of(b * BLK, BLK), BLK)
        hit = hits(b)
        g = (et[rows, :] * inverse - jnp.where(hit, 1.0, 0.0)) * logit_scale
        gt[rows, :] = g.astype(jnp.bfloat16)
        return carry

    def center_part(half, k):
        q = half * 2 + k
        return jnp.dot(gt[q * 256:(q + 1) * 256, :], xv, preferred_element_type=jnp.float32)

    given = 0

    def give(d, dst, rsem, dev):
        nonlocal given
        send(part_b.at[AT[d % NZ]], dst, r_send.at[given], rsem, dev)
        given += 1

    def other_part(k):
        lax.fori_loop(32 + k * 16, 48 + k * 16, grad, 0)
        sib_out[k * 8:k * 8 + 8] = center_part(1, k).astype(jnp.bfloat16).reshape(8, CLS, D)
        send(sib_out.at[pl.ds(k * 8, 8)], sib_in.at[pl.ds(k * 8, 8)], cs_send.at[k], cs_recv.at[k], sibling)

    def own_part(k):
        lax.fori_loop(k * 16, k * 16 + 16, grad, 0)
        part[k * 8:k * 8 + 8] = center_part(0, k).reshape(8, CLS, D)

    def add_up(k):
        arrived(sib_in.at[pl.ds(k * 8, 8)], cs_send.at[k], cs_recv.at[k], sibling)
        p = part[k * 8:k * 8 + 8] + sib_in[k * 8:k * 8 + 8].astype(jnp.float32)
        part[k * 8:k * 8 + 8] = p
        part_b[k * 8:k * 8 + 8] = p.astype(jnp.bfloat16)

    other_part(1)
    own_part(1)
    other_part(0)
    add_up(1)
    give(8, near8.at[...], r_recv.at[4], (wrap(z - 2 * up, NZ), cls))
    for side, s in ((0, 1), (1, -1)):
        give(-7 * s, near6.at[side, 1], r_recv.at[side * 2 + 1], zdev(-s))
        give(-5 * s, near6.at[side, 0], r_recv.at[side * 2], zdev(s))
    for side, s in ((0, 1), (1, -1)):
        give(-4 * s, near3.at[side, 1], r_recv.at[6 + side * 2], zdev(-s))

    column = jnp.transpose(jnp.broadcast_to(inverse, (8, TILE_ROWS)))[:, :1]
    fsum = (fval[...] * column - hval[...]) * logit_scale
    fval[...] = fsum
    fout[...] = fsum.astype(jnp.bfloat16).reshape(NP, ROWS, D)
    for i in (1, 2, 3, 0):
        for j in (2, 1, 3):
            slot = chip(wrap(first + i, SIDE), wrap(second + j, SIDE))
            send(fout.at[slot], fin1.at[SIDE - j, i], f_send.at[j, i], f_recv.at[SIDE - j, i],
                 pdev(chip(first, wrap(second + j, SIDE))))

    own_part(0)
    add_up(0)
    for side, s in ((0, 1), (1, -1)):
        give(-2 * s, near3.at[side, 0], r_recv.at[5 + side * 2], zdev(s))
    for side, s in ((0, 1), (1, -1)):
        give(s, zfin.at[side], q_recv.at[side], zdev(s))
    for j in range(1, NP):
        send(tgt.at[0], tgt.at[NP - j], u_send.at[j], u_recv.at[NP - j], pdev(wrap(yx + j, NP)))

    before = len(started)

    arrived(near8.at[...], r_send.at[0], r_recv.at[4], (wrap(z + 2 * up, NZ), cls))
    for side, s in ((0, 1), (1, -1)):
        arrived(near6.at[side, 0], r_send.at[0], r_recv.at[side * 2], zdev(-s))
        arrived(near6.at[side, 1], r_send.at[0], r_recv.at[side * 2 + 1], zdev(s))
        acc = part[AT[-6 * s % NZ]] + near6[side, 0].astype(jnp.float32) + near6[side, 1].astype(jnp.float32)
        acc = acc + jnp.where(core == side, near8[...].astype(jnp.float32), 0.0)
        out6[side] = acc.astype(jnp.bfloat16)
        send(out6.at[side], zfin.at[4 + side], q_send.at[side], q_recv.at[4 + side], zdev(-6 * s))

    for side, s in ((0, 1), (1, -1)):
        arrived(near3.at[side, 0], r_send.at[0], r_recv.at[5 + side * 2], zdev(-s))
        arrived(near3.at[side, 1], r_send.at[0], r_recv.at[6 + side * 2], zdev(s))
        acc = part[AT[-3 * s % NZ]] + near3[side, 0].astype(jnp.float32) + near3[side, 1].astype(jnp.float32)
        out3[side] = acc.astype(jnp.bfloat16)
        send(out3.at[side], zfin.at[2 + side], q_send.at[2 + side], q_recv.at[2 + side], zdev(-3 * s))

    last = started[before:]
    del started[before:]

    own_f = None
    for i in (1, 2, 3, 0):
        slot = chip(wrap(first + i, SIDE), second)
        acc = fval[pl.ds(pl.multiple_of(slot * ROWS, 16), ROWS), :]
        for j in (1, 2, 3):
            arrived(fin1.at[j, i], f_send.at[j, i], f_recv.at[j, i], pdev(chip(first, wrap(second + j, SIDE))))
            acc = acc + fin1[j, i].astype(jnp.float32)
        if i:
            fout2[i] = acc.astype(jnp.bfloat16)
            send(fout2.at[i], fin2.at[SIDE - i], h_send.at[i], h_recv.at[SIDE - i], pdev(slot))
        else:
            own_f = acc

    for j in range(1, NP):
        arrived(tgt.at[j], u_send.at[j], u_recv.at[j], pdev(wrap(yx + j, NP)))
    target = tgt[0]
    for j in range(1, NP):
        target = target + tgt[j]
    every = jnp.log(total) - target
    own_loss = every[:, :ROWS]
    for k in range(1, NP):
        own_loss = jnp.where(yx == k, every[:, k * ROWS:(k + 1) * ROWS], own_loss)
    loss_ref[...] = own_loss

    def back(v, q, g):
        return g * q - v * (q * q * q * jnp.sum(v * g, axis=-1, keepdims=True))

    for i in (1, 2, 3):
        arrived(fin2.at[i], h_send.at[i], h_recv.at[i], pdev(chip(wrap(first + i, SIDE), second)))
        own_f = own_f + fin2[i].astype(jnp.float32)
    fgrad_ref[...] = back(v, fq, own_f)

    for copy in started:
        copy.wait_send()
    own_c = part[0]
    for i, d in enumerate((-1, 1, 3, -3, 6, -6)):
        arrived(zfin.at[i], q_send.at[0], q_recv.at[i], zdev(d))
        own_c = own_c + zfin[i].astype(jnp.float32)
    cgrad_ref[...] = back(c, cq, own_c)

    for copy in last:
        copy.wait_send()


def hand_over(a_ref, b_ref, c_ref, a_out, b_out, c_out):
    a_out[...] = a_ref[...]
    b_out[...] = b_ref[...]
    c_out[...] = c_ref[...]


def scratch():
    bf, f32, dma = jnp.bfloat16, jnp.float32, pltpu.SemaphoreType.DMA
    vm = pltpu.VMEM
    return [
        vm((ROWS, D), bf), vm((BLOCKS, BLK, D), f32), vm((192, 128), jnp.int32),
        pltpu.SMEM((2, 2 * NZ * NP), jnp.int32), pltpu.SMEM((64,), jnp.int32),
        vm((CLS, D), f32), vm((NP, ROWS, D), bf), vm((2, NZ, CLS, D), bf),
        vm((TILE_CLS, TILE_ROWS), f32), vm((TILE_CLS, TILE_ROWS), bf), vm((TILE_ROWS, 128), jnp.int32),
        vm((256, 512), f32), vm((256, 512), bf), vm((256, 512), bf),
        vm((NP, 1, TILE_ROWS), f32), vm((NP, 1, TILE_ROWS), f32),
        vm((NZ, CLS, D), bf), vm((NZ, CLS, D), bf), vm((NZ, CLS, D), f32), vm((NZ, CLS, D), bf),
        vm((2, 2, CLS, D), bf), vm((CLS, D), bf), vm((2, 2, CLS, D), bf),
        vm((2, CLS, D), bf), vm((2, CLS, D), bf), vm((6, CLS, D), bf),
        vm((TILE_ROWS, D), f32), vm((TILE_ROWS, D), f32), vm((NP, ROWS, D), bf), vm((SIDE, SIDE, ROWS, D), bf),
        vm((SIDE, ROWS, D), bf), vm((SIDE, ROWS, D), bf),
        dma((7,)), dma((NZ,)), dma((NZ,)), dma((NZ,)), dma((NZ,)), dma((SIDE,)), dma((SIDE,)),
        dma((SIDE, SIDE)), dma((SIDE, SIDE)),
        dma((NP,)), dma((NP,)), dma((NP,)), dma((NP,)), dma((2,)), dma((2,)),
        dma((11,)), dma((9,)), dma((4,)), dma((6,)), dma((SIDE, SIDE)), dma((SIDE, SIDE)), dma((SIDE,)), dma((SIDE,)),
    ]


def local(features, centers, labels, sampled):
    hbm = pl.BlockSpec(memory_space=pltpu.HBM)
    vmem = pl.BlockSpec(memory_space=pltpu.VMEM)
    losses, feature_grad, center_grad = pl.pallas_call(
        kernel,
        out_shape=(
            jax.ShapeDtypeStruct((1, ROWS), jnp.float32),
            jax.ShapeDtypeStruct((ROWS, D), jnp.float32),
            jax.ShapeDtypeStruct((CLS, D), jnp.float32),
        ),
        in_specs=[hbm, hbm, hbm, hbm],
        out_specs=(vmem, vmem, vmem),
        scratch_shapes=scratch(),
        compiler_params=pltpu.CompilerParams(
            collective_id=0, has_side_effects=True, vmem_limit_bytes=62 * 1024 * 1024
        ),
        name="margin_step",
    )(features, centers.reshape(BLOCKS, BLK, D), labels.reshape(192, 128), sampled.T)
    losses, feature_grad, center_grad = pl.pallas_call(
        hand_over,
        out_shape=(
            jax.ShapeDtypeStruct((1, ROWS), jnp.float32),
            jax.ShapeDtypeStruct((ROWS, D), jnp.float32),
            jax.ShapeDtypeStruct((CLS, D), jnp.float32),
        ),
        in_specs=[vmem] * 3,
        out_specs=(vmem,) * 3,
        compiler_params=pltpu.CompilerParams(vmem_limit_bytes=62 * 1024 * 1024),
        name="hand_over",
    )(losses, feature_grad, center_grad)
    return (losses.reshape(ROWS), feature_grad, center_grad)


def solution(mesh):
    placed = (P(("dp", "cls"), None), P(("dp", "cls"), None), P(), P())
    return jax.shard_map(
        local,
        mesh=mesh,
        in_specs=placed,
        out_specs=(P(("dp", "cls")), P(("dp", "cls"), None), P(("dp", "cls"), None)),
        check_vma=False,
    )
```
